32 devices in a mesh: tm: 8 (over z, y), space: 4 (over x, core).
Axes of the slice: x: 2, y: 2, z: 4, core: 2. Of those that a mesh axis runs over, the one named last changes fastest.
Arguments:
- prior_adjoint_iterate: float32 [8, 64, 128, 128], P('tm', 'space'), may hold values from -6 to 6
- material: int32 [64, 128, 128], P('space'), may hold values from 0 to 7
- probe_cell_index: int32 [256], P('space'), may hold values from 0 to 1048575, as said below
- misfit: float32 [8, 256], P('tm', 'space'), may hold values from -12 to 12
- ventilation_heat_loss: float32 [8], P('tm'), as said below
- conductance: float32 [8], replicated, may hold values from 0.03 to 0.14
- rock_heat_drain: float32 [8], replicated, as said below
Outputs:
- adjoint_new: float32 [8, 64, 128, 128], P('tm', 'space')
The draws below stay inside these ranges and needn't reach their ends.
Inputs may be any that keep to these rules, and one draw needn't show every extreme that they name: `probe_cell_index`: sensors 64 p to 64 (p + 1) - 1 lie in the p-th block of 16 planes of the first dimension; a cell may hold several sensors. `ventilation_heat_loss`: Non-negative. `rock_heat_drain`: Positive.
All inputs are finite; a program needn't handle non-finite values.
Results may differ from the reference program's by a relative error of at most 0.00002.
Values sent between devices are 32-bit elements; how exact they have to be, the bound alone decides.
A program may use at most 64 MiB of HBM per device.

```python
import math
import jax
import jax.numpy as jnp

CX = 16
NY = 128
NZ = 128
FINE_STEPS = 4
MATS = 8
SENS_DEV = 64
SLABS = 8
NX = 64
SENS = 256


def draw_probe_cell_index(key, part):
    number = jnp.arange(SENS, dtype=jnp.int32)
    tiles = number // SENS_DEV
    offset = jax.random.randint(key, (SENS,), 0, CX * NY * NZ, dtype=jnp.int32)
    offset = jnp.where(number == 0, 0, offset)
    offset = jnp.where(number == SENS - 1, CX * NY * NZ - 1, offset)
    return (tiles * (CX * NY * NZ) + offset).astype(jnp.int32)


def draw_rock_heat_drain(key, part):
    spread = jax.random.uniform(jax.random.fold_in(key, 11), (MATS,), jnp.float32)
    lower, upper = (0.0001, 0.06)
    return jnp.exp(jnp.log(lower) + spread * (jnp.log(upper) - jnp.log(lower))).astype(jnp.float32)


def draw_ventilation_heat_loss(key, part):
    count = max(1, SLABS // 8)
    order = jax.random.permutation(jax.random.fold_in(key, 21), SLABS)
    strength = jax.random.uniform(jax.random.fold_in(key, 22), (SLABS,), jnp.float32, 0.05, 0.15)
    return jnp.where(order < count, strength, 0.0).astype(jnp.float32)


def plant(result, rng, least, high):
    longest = result.shape.index(max(result.shape))
    spots = []
    for shift in (0, 1):
        where = [jax.random.randint(jax.random.fold_in(rng, axis), (), 0, length) for axis, length in enumerate(result.shape)]
        where[longest] = (where[longest] + shift) % result.shape[longest]
        spots.append(tuple(where))
    return result.at[spots[0]].set(least).at[spots[1]].set(high)


def block_levels(key, dims, pieces, least, largest):
    def one(dim, shards_of):
        heights = jax.random.uniform(jax.random.fold_in(jax.random.fold_in(key, 6), dim), (shards_of,), jnp.float32, least / len(pieces), largest / len(pieces))
        return jnp.repeat(jnp.exp(heights), dims[dim] // shards_of).reshape((-1,) + (1,) * (len(dims) - dim - 1))

    factor_of = one(*pieces[0])
    for cut in pieces[1:]:
        factor_of = factor_of * one(*cut)
    return factor_of


def noise(own_key, dims, deviation, bound, cuts=(), held_as=jnp.bfloat16):
    values = jax.random.normal(own_key, dims, jnp.float32) * deviation
    if len(cuts) > 0:
        values = block_levels(own_key, dims, cuts, -0.22, 0.18) * values
    return jnp.clip(values, min=-bound, max=bound).astype(held_as)


def setup_inputs(seed: int = 0) -> dict:
    streams_of = jax.random.split(jax.random.key(seed), 8)
    prior_adjoint_iterate = noise(streams_of[0], (SLABS, NX, NY, NZ), 1.0, 6.0, ((0, 8), (1, 4)), jnp.float32)
    material = plant(jax.random.randint(streams_of[1], (NX, NY, NZ), 0, MATS), jax.random.fold_in(streams_of[1], 1), 0, MATS - 1).astype(jnp.int32)
    probe_cell_index = draw_probe_cell_index(jax.random.fold_in(streams_of[7], 71), 0)
    misfit = noise(streams_of[3], (SLABS, SENS), 2.0, 12.0, ((0, 8), (1, 4)), jnp.float32)
    ventilation_heat_loss = draw_ventilation_heat_loss(jax.random.fold_in(streams_of[7], 71), 0)
    conductance = jnp.clip(jnp.exp(jax.random.uniform(streams_of[5], (MATS,), jnp.float32, math.log(0.03), math.log(0.14))), 0.03, 0.14)
    rock_heat_drain = draw_rock_heat_drain(jax.random.fold_in(streams_of[7], 71), 0)
    return {"prior_adjoint_iterate": prior_adjoint_iterate, "material": material, "probe_cell_index": probe_cell_index, "misfit": misfit, "ventilation_heat_loss": ventilation_heat_loss, "conductance": conductance, "rock_heat_drain": rock_heat_drain}


def coarsen(field):
    split = field.reshape(field.shape[0] // 2, 2, field.shape[1] // 2, 2, field.shape[2])
    return 0.25 * ((split[:, 0, :, 0] + split[:, 1, :, 0]) + (split[:, 0, :, 1] + split[:, 1, :, 1]))


def refine(coarse):
    return jnp.repeat(jnp.repeat(coarse, 2, axis=0), 2, axis=1)


def neighbours(padded):
    x_sides = padded[2:, 1:-1, 1:-1] + padded[:-2, 1:-1, 1:-1]
    y_sides = padded[1:-1, 2:, 1:-1] + padded[1:-1, :-2, 1:-1]
    z_sides = padded[1:-1, 1:-1, 2:] + padded[1:-1, 1:-1, :-2]
    return (x_sides + y_sides) + z_sides


def reference(prior_adjoint_iterate, material, probe_cell_index, misfit, ventilation_heat_loss, conductance, rock_heat_drain):
    cond_cell = conductance[material]
    cell_heat_drain = rock_heat_drain[material]
    coarse_heat_drain = coarsen(cell_heat_drain)
    rates = []
    corrections = []
    for window_index in range(SLABS):
        source = jnp.zeros((NX * NY * NZ,), jnp.float32).at[probe_cell_index].add(misfit[window_index]).reshape(NX, NY, NZ)
        drain_amounts = cell_heat_drain + ventilation_heat_loss[window_index]
        current = prior_adjoint_iterate[window_index] + source
        for sweep_index in range(FINE_STEPS):
            weighted = cond_cell * current
            current = current + (neighbours(jnp.pad(weighted, 1)) - 6.0 * weighted) - drain_amounts * current
        coarse_decay_rate = jnp.exp(-FINE_STEPS * (coarse_heat_drain + ventilation_heat_loss[window_index]))
        correction = current - refine(coarse_decay_rate * coarsen(prior_adjoint_iterate[window_index]))
        rates.append(coarse_decay_rate)
        corrections.append(correction)
    chained = coarsen(prior_adjoint_iterate[SLABS - 1])
    outputs = [None] * SLABS
    for window_index in reversed(range(SLABS)):
        outputs[window_index] = refine(rates[window_index] * chained) + corrections[window_index]
        chained = rates[window_index] * chained + coarsen(corrections[window_index])
    return jnp.stack(outputs)
```

```python
import functools

import jax
import jax.numpy as jnp
from jax import lax
from jax.experimental import pallas as pl
from jax.experimental.pallas import tpu as pltpu
from jax.sharding import PartitionSpec as P

FINE_STEPS = 4
PAD = 8
F32 = jnp.float32
BF16 = jnp.bfloat16


def lookup(rock, tables):
    bits = [(rock & (1 << b)) != 0 for b in range(3)]
    found = []
    for table in tables:
        level = table
        for bit in bits:
            level = [jnp.where(bit, level[2 * n + 1], level[2 * n]) for n in range(len(level) // 2)]
        found.append(level[0])
    return found


def kernel(
    slabs, tiles,
    prior, material, probe, misfit, vent, conductance, drain,
    out,
    w, cond, keep, loss, rate, old, red,
    seen, mate_vent, my_vent, mate_red, gain, base, high_red, high_rate,
    chain_in, chain_out, swap_out, swap_in,
    vent_sem, halo_send, halo_recv, red_send, red_recv, chain_send, chain_recv, swap_send, swap_recv,
):
    t, p = lax.axis_index("tm"), lax.axis_index("space")
    planes, across, depth = prior.shape[1:]
    coarse = planes // 2
    half = coarse // 2
    rows = pl.ds(PAD, across)
    low = lax.rem(t, 2) == 0
    mate = jnp.where(low, t + 1, t - 1)
    has_lower, has_upper = t >= 2, t < slabs - 2
    has_left, has_right = p > 0, p < tiles - 1
    is_top = t == slabs - 1

    def own_plane(k):
        return jnp.where(low, half - 1 - k, half + k)

    def mate_plane(k):
        return jnp.where(low, half + k, half - 1 - k)

    barrier = pltpu.get_barrier_semaphore()

    def greet(axis, index):
        pl.semaphore_signal(barrier, inc=1, device_id={axis: index}, device_id_type=pl.DeviceIdType.MESH)

    greet("tm", mate)
    pl.when(has_lower)(lambda: greet("tm", t - 2))
    pl.when(has_upper)(lambda: greet("tm", t + 2))
    pl.when(has_left)(lambda: greet("space", p - 1))
    pl.when(has_right)(lambda: greet("space", p + 1))

    def send(src, dst, send_sem, recv_sem, axis, index):
        return pltpu.make_async_remote_copy(
            src_ref=src, dst_ref=dst, send_sem=send_sem, recv_sem=recv_sem,
            device_id={axis: index}, device_id_type=pl.DeviceIdType.MESH,
        )

    def vent_copy():
        return send(my_vent, mate_vent, vent_sem.at[0], vent_sem.at[1], "tm", mate)

    def left_copy(n):
        return send(w.at[n, 1, rows], w.at[n, planes + 1, rows], halo_send.at[n, 0], halo_recv.at[n, 0], "space", p - 1)

    def right_copy(n):
        return send(w.at[n, planes, rows], w.at[n, 0, rows], halo_send.at[n, 1], halo_recv.at[n, 1], "space", p + 1)

    def red_copy(k):
        return send(red.at[mate_plane(k)], mate_red.at[k], red_send.at[k], red_recv.at[k], "tm", mate)

    def chain_copy(k):
        return send(chain_out.at[k], chain_in.at[k], chain_send.at[k], chain_recv.at[k], "tm", t - 2)

    def swap_copy(k):
        return send(swap_out.at[k], swap_in.at[k], swap_send.at[k], swap_recv.at[k], "tm", mate)

    extra = vent[0]
    cond_of = [conductance[m] for m in range(conductance.shape[0])]
    drain_of = [drain[m] for m in range(drain.shape[0])]

    cell = probe[...] - p * (planes * across * depth)
    cell_row, cell_lane = cell // depth, lax.rem(cell, depth)
    amount = misfit[...]
    first = amount.astype(BF16)
    rest = amount - first.astype(F32)
    second = rest.astype(BF16)
    third = rest - second.astype(F32)
    place = lax.broadcasted_iota(jnp.int32, (depth, cell.shape[1]), 0) == cell_lane
    for n, term in enumerate((first.astype(F32), second.astype(F32), third)):
        seen[n] = jnp.where(place, term, 0.0).astype(BF16)

    def seed(i):
        number = lax.broadcasted_iota(jnp.int32, (across, cell.shape[1]), 0) + i * across
        hit = jnp.where(number == cell_row, 1.0, 0.0).astype(BF16)
        added = sum(
            lax.dot_general(hit, seen[n], (((1,), (1,)), ((), ())), preferred_element_type=F32)
            for n in range(3)
        )
        c, l = lookup(material[i], (cond_of, drain_of))
        cond[i] = c
        loss[i] = l
        keep[i] = 1.0 - 6.0 * c - (l + extra)
        w[0, i + 1, rows] = c * (prior[0, i] + added)

    edge = jnp.zeros((PAD, depth), F32)

    def clear(i, _):
        for n in range(FINE_STEPS):
            w[n, i + 1, pl.ds(0, PAD)] = edge
            w[n, i + 1, pl.ds(PAD + across, PAD)] = edge
        return 0

    lax.fori_loop(0, planes, clear, 0)
    seed(0)
    seed(planes - 1)
    my_vent[...] = jnp.full(my_vent.shape, extra, F32)

    @pl.when(jnp.logical_not(has_left))
    def _():
        for n in range(FINE_STEPS):
            w[n, 0, rows] = jnp.zeros((across, depth), F32)

    @pl.when(jnp.logical_not(has_right))
    def _():
        for n in range(FINE_STEPS):
            w[n, planes + 1, rows] = jnp.zeros((across, depth), F32)

    @pl.when(jnp.logical_not(has_upper))
    def _():
        chain_in[...] = jnp.zeros(chain_in.shape, F32)

    count = 1 + has_lower.astype(jnp.int32) + has_upper.astype(jnp.int32)
    count = count + has_left.astype(jnp.int32) + has_right.astype(jnp.int32)
    pl.semaphore_wait(barrier, count)

    def send_faces(n):
        pl.when(has_left)(lambda: left_copy(n).start())
        pl.when(has_right)(lambda: right_copy(n).start())

    def wait_faces(n):
        pl.when(has_right)(lambda: left_copy(n).wait_recv())
        pl.when(has_left)(lambda: right_copy(n).wait_recv())

    send_faces(0)
    vent_copy().start()

    lax.fori_loop(1, planes - 1, lambda i, c: (seed(i), c)[1], 0)

    def four(ref, q):
        even, odd = pl.ds(0, across // 2, stride=2), pl.ds(1, across // 2, stride=2)
        a, b = ref.at[2 * q], ref.at[2 * q + 1]
        return 0.25 * ((a[even, :] + b[even, :]) + (a[odd, :] + b[odd, :]))

    def prepare(q, _):
        rate[q] = jnp.exp(-FINE_STEPS * (four(loss, q) + extra))
        old[q] = four(prior.at[0], q)
        return 0

    lax.fori_loop(0, coarse, prepare, 0)

    lane = lax.broadcasted_iota(jnp.int32, (across, depth), 1)

    def around(n, i):
        here = w[n, i + 1, rows]
        x_sides = w[n, i, rows] + w[n, i + 2, rows]
        y_sides = w[n, i + 1, pl.ds(PAD - 1, across)] + w[n, i + 1, pl.ds(PAD + 1, across)]
        before = jnp.where(lane == 0, 0.0, pltpu.roll(here, 1, 1))
        after = jnp.where(lane == depth - 1, 0.0, pltpu.roll(here, depth - 1, 1))
        return here, x_sides + y_sides + (before + after)

    def step(n, i):
        here, sides = around(n, i)
        w[n + 1, i + 1, rows] = keep[i] * here + cond[i] * sides

    for n in range(FINE_STEPS - 1):
        wait_faces(n)
        step(n, 0)
        step(n, planes - 1)
        send_faces(n + 1)
        lax.fori_loop(1, planes - 1, lambda i, c: (step(n, i), c)[1], 0)

    def finish(i):
        here, sides = around(FINE_STEPS - 1, i)
        out[0, i] = keep[i] * here / cond[i] + sides

    def reduce(q):
        mean = four(out.at[0], q)
        red[q] = jnp.where(is_top, mean, mean - rate[q] * old[q])

    def last_step(k):
        for q in (half - 1 - k, half + k):
            finish(2 * q)
            finish(2 * q + 1)
            reduce(q)
        red_copy(k).start()

    lax.fori_loop(0, half - 1, lambda k, c: (last_step(k), c)[1], 0)
    wait_faces(FINE_STEPS - 1)
    last_step(half - 1)
    vent_copy().wait_recv()

    def combine(k, _):
        q = own_plane(k)
        mine = rate[q]
        his = jnp.exp(-FINE_STEPS * (four(loss, q) + mate_vent[0:1, :]))
        red_copy(k).wait_recv()
        low_rate, upper_rate = jnp.where(low, mine, his), jnp.where(low, his, mine)
        low_red, upper_red = jnp.where(low, red[q], mate_red[k]), jnp.where(low, mate_red[k], red[q])
        gain[k] = low_rate * upper_rate
        base[k] = low_red + low_rate * upper_red
        high_red[k] = upper_red
        high_rate[k] = upper_rate
        return 0

    lax.fori_loop(0, half, combine, 0)

    def add_carry(q, carry):
        moved = jnp.where(is_top, 0.0, rate[q] * (carry - old[q]))
        for i in (2 * q, 2 * q + 1):
            plane = out.at[0, i]
            for phase in range(2):
                pick = pl.ds(phase, across // 2, stride=2)
                plane[pick, :] = plane[pick, :] + moved

    def link(k, _):
        pl.when(has_upper)(lambda: chain_copy(k).wait_recv())
        entering = chain_in[k]
        chain_out[k] = base[k] + gain[k] * entering
        pl.when(has_lower)(lambda: chain_copy(k).start())
        lower = high_red[k] + high_rate[k] * entering
        swap_out[k] = jnp.where(low, entering, lower)
        swap_copy(k).start()
        add_carry(own_plane(k), jnp.where(low, lower, entering))
        return 0

    lax.fori_loop(0, half, link, 0)

    def close(k, _):
        swap_copy(k).wait_recv()
        add_carry(mate_plane(k), swap_in[k])
        return 0

    lax.fori_loop(0, half, close, 0)

    vent_copy().wait_send()
    for n in range(FINE_STEPS):
        pl.when(has_left)(lambda: left_copy(n).wait_send())
        pl.when(has_right)(lambda: right_copy(n).wait_send())
    for k in range(half):
        red_copy(k).wait_send()
        pl.when(has_lower)(lambda: chain_copy(k).wait_send())
        swap_copy(k).wait_send()


def on_device(slabs, tiles, prior, material, probe, misfit, vent, conductance, drain):
    planes, across, depth = prior.shape[1:]
    coarse, half = planes // 2, planes // 4
    sensors = probe.shape[0]
    vmem, smem = pl.BlockSpec(memory_space=pltpu.VMEM), pl.BlockSpec(memory_space=pltpu.SMEM)
    whole = pltpu.VMEM((planes, across, depth), F32)
    quarter = pltpu.VMEM((coarse, across // 2, depth), F32)
    eighth = pltpu.VMEM((half, across // 2, depth), F32)
    small = pltpu.VMEM((8, depth), F32)
    dma = pltpu.SemaphoreType.DMA
    return pl.pallas_call(
        functools.partial(kernel, slabs, tiles),
        out_shape=jax.ShapeDtypeStruct(prior.shape, F32),
        in_specs=[vmem, vmem, vmem, vmem, smem, smem, smem],
        out_specs=vmem,
        scratch_shapes=[
            pltpu.VMEM((FINE_STEPS, planes + 2, across + 2 * PAD, depth), F32),
            whole, whole, whole, quarter, quarter, quarter,
            pltpu.VMEM((3, depth, sensors), BF16),
            small, small, eighth, eighth, eighth, eighth, eighth,
            eighth, eighth, eighth, eighth,
            dma((2,)), dma((FINE_STEPS, 2)), dma((FINE_STEPS, 2)),
            dma((half,)), dma((half,)), dma((half,)), dma((half,)), dma((half,)), dma((half,)),
        ],
        compiler_params=pltpu.CompilerParams(
            collective_id=0, has_side_effects=True, vmem_limit_bytes=48 * 1024 * 1024
        ),
    )(prior, material, probe.reshape(1, sensors), misfit, vent, conductance, drain)


def solution(mesh):
    in_specs = (
        P("tm", "space", None, None),
        P("space", None, None),
        P("space"),
        P("tm", "space"),
        P("tm"),
        P(),
        P(),
    )
    out_specs = P("tm", "space", None, None)
    run = functools.partial(on_device, mesh.shape["tm"], mesh.shape["space"])
    return jax.shard_map(run, mesh=mesh, in_specs=in_specs, out_specs=out_specs, check_vma=False)
```

```python
import functools

import jax
import jax.numpy as jnp
from jax import lax
from jax.experimental import pallas as pl
from jax.experimental.pallas import tpu as pltpu
from jax.sharding import PartitionSpec as P

FINE_STEPS = 4
PAD = 8
CUT = 2
UNROLL = 2
F32 = jnp.float32
BF16 = jnp.bfloat16


def lookup(rock, tables):
    bits = [(rock & (1 << b)) != 0 for b in range(3)]
    found = []
    for table in tables:
        level = table
        for bit in bits:
            level = [jnp.where(bit, level[2 * n + 1], level[2 * n]) for n in range(len(level) // 2)]
        found.append(level[0])
    return found


def kernel(
    slabs, tiles,
    prior_in, material_in, probe_in, misfit_in, vent_in, conductance_in, drain_in,
    out,
    prior, material, probe, misfit, vent, conductance, drain, in_sem,
    w, cond, keep, loss, rate, old, red,
    seen, mate_vent, my_vent, mate_red, gain, base, high_red, high_rate,
    chain_in, chain_out, swap_out, swap_in, carried,
    vent_sem, halo_send, halo_recv, red_send, red_recv, chain_send, chain_recv, swap_send, swap_recv,
):
    t, p = lax.axis_index("tm"), lax.axis_index("space")
    planes, across, depth = prior.shape[1:]
    coarse = planes // 2
    half = coarse // 2
    chunks = half * CUT
    part = across // 2 // CUT
    inner = pl.ds(1, planes - 2)
    small = [(probe_in, probe), (misfit_in, misfit), (vent_in, vent), (conductance_in, conductance), (drain_in, drain)]
    faces, body = [], []
    for i in (0, planes - 1):
        faces += [(prior_in.at[0, i], prior.at[0, i]), (material_in.at[i], material.at[i])]
    body += [(material_in.at[inner], material.at[inner]), (prior_in.at[0, inner], prior.at[0, inner])]
    loads = [pltpu.make_async_copy(a, b, in_sem.at[n]) for n, (a, b) in enumerate(small + faces + body)]
    for load in loads:
        load.start()
    rows = pl.ds(PAD, across)
    low = lax.rem(t, 2) == 0
    mate = jnp.where(low, t + 1, t - 1)
    has_lower, has_upper = t >= 2, t < slabs - 2
    has_left, has_right = p > 0, p < tiles - 1
    is_top = t == slabs - 1

    def own_chunk(c):
        k, r = c // CUT, c % CUT
        return jnp.where(low, half - 1 - k, half + k) * CUT + r

    def mate_chunk(c):
        k, r = c // CUT, c % CUT
        return jnp.where(low, half + k, half - 1 - k) * CUT + r

    barrier = pltpu.get_barrier_semaphore()

    def greet(axis, index):
        pl.semaphore_signal(barrier, inc=1, device_id={axis: index}, device_id_type=pl.DeviceIdType.MESH)

    greet("tm", mate)
    pl.when(has_lower)(lambda: greet("tm", t - 2))
    pl.when(has_upper)(lambda: greet("tm", t + 2))
    pl.when(has_left)(lambda: greet("space", p - 1))
    pl.when(has_right)(lambda: greet("space", p + 1))

    def send(src, dst, send_sem, recv_sem, axis, index):
        return pltpu.make_async_remote_copy(
            src_ref=src, dst_ref=dst, send_sem=send_sem, recv_sem=recv_sem,
            device_id={axis: index}, device_id_type=pl.DeviceIdType.MESH,
        )

    def vent_copy():
        return send(my_vent, mate_vent, vent_sem.at[0], vent_sem.at[1], "tm", mate)

    def left_copy(n):
        return send(w.at[n, 1, rows], w.at[n, planes + 1, rows], halo_send.at[n, 0], halo_recv.at[n, 0], "space", p - 1)

    def right_copy(n):
        return send(w.at[n, planes, rows], w.at[n, 0, rows], halo_send.at[n, 1], halo_recv.at[n, 1], "space", p + 1)

    def red_copy(k):
        return send(red.at[mate_chunk(k)], mate_red.at[k], red_send.at[k], red_recv.at[k], "tm", mate)

    def chain_copy(k):
        return send(chain_out.at[k], chain_in.at[k], chain_send.at[k], chain_recv.at[k], "tm", t - 2)

    def swap_copy(k):
        return send(swap_out.at[k], swap_in.at[k], swap_send.at[k], swap_recv.at[k], "tm", mate)

    edge = jnp.zeros((PAD, depth), F32)

    def clear(i, _):
        for n in range(FINE_STEPS):
            w[n, i + 1, pl.ds(0, PAD)] = edge
            w[n, i + 1, pl.ds(PAD + across, PAD)] = edge
        return 0

    lax.fori_loop(0, planes, clear, 0)

    @pl.when(jnp.logical_not(has_left))
    def _():
        for n in range(FINE_STEPS):
            w[n, 0, rows] = jnp.zeros((across, depth), F32)

    @pl.when(jnp.logical_not(has_right))
    def _():
        for n in range(FINE_STEPS):
            w[n, planes + 1, rows] = jnp.zeros((across, depth), F32)

    for load in loads[: len(small)]:
        load.wait()
    extra = vent[0]
    cond_of = [conductance[m] for m in range(conductance.shape[0])]
    drain_of = [drain[m] for m in range(drain.shape[0])]

    cell = probe[...] - p * (planes * across * depth)
    cell_row, cell_lane = cell // depth, lax.rem(cell, depth)
    amount = misfit[...]
    first = amount.astype(BF16)
    rest = amount - first.astype(F32)
    second = rest.astype(BF16)
    third = rest - second.astype(F32)
    place = lax.broadcasted_iota(jnp.int32, (depth, cell.shape[1]), 0) == cell_lane
    for n, term in enumerate((first.astype(F32), second.astype(F32), third)):
        seen[n] = jnp.where(place, term, 0.0).astype(BF16)

    def seed(i):
        number = lax.broadcasted_iota(jnp.int32, (across, cell.shape[1]), 0) + i * across
        hit = jnp.where(number == cell_row, 1.0, 0.0).astype(BF16)
        added = sum(
            lax.dot_general(hit, seen[n], (((1,), (1,)), ((), ())), preferred_element_type=F32)
            for n in range(3)
        )
        c, l = lookup(material[i], (cond_of, drain_of))
        cond[i] = c
        loss[i] = l
        keep[i] = 1.0 - 6.0 * c - (l + extra)
        w[0, i + 1, rows] = c * (prior[0, i] + added)

    for load in loads[len(small) : len(small) + len(faces)]:
        load.wait()
    seed(0)
    seed(planes - 1)
    my_vent[...] = jnp.full(my_vent.shape, extra, F32)
    count = 1 + has_lower.astype(jnp.int32) + has_upper.astype(jnp.int32)
    count = count + has_left.astype(jnp.int32) + has_right.astype(jnp.int32)
    pl.semaphore_wait(barrier, count)

    def send_faces(n):
        pl.when(has_left)(lambda: left_copy(n).start())
        pl.when(has_right)(lambda: right_copy(n).start())

    def wait_faces(n):
        pl.when(has_right)(lambda: left_copy(n).wait_recv())
        pl.when(has_left)(lambda: right_copy(n).wait_recv())

    send_faces(0)
    vent_copy().start()

    for load in loads[len(small) + len(faces) :]:
        load.wait()
    lax.fori_loop(1, planes - 1, lambda i, c: (seed(i), c)[1], 0, unroll=2)

    def four(ref, j):
        q, r = j // CUT, j % CUT
        start = 2 * part * r
        even, odd = pl.ds(start, part, stride=2), pl.ds(start + 1, part, stride=2)
        a, b = ref.at[2 * q], ref.at[2 * q + 1]
        return 0.25 * ((a[even, :] + b[even, :]) + (a[odd, :] + b[odd, :]))

    def prepare(j, _):
        rate[j] = jnp.exp(-FINE_STEPS * (four(loss, j) + extra))
        old[j] = four(prior.at[0], j)
        return 0

    lax.fori_loop(0, coarse * CUT, prepare, 0, unroll=2)

    lane = lax.broadcasted_iota(jnp.int32, (across, depth), 1)

    def around(n, i):
        here = w[n, i + 1, rows]
        x_sides = w[n, i, rows] + w[n, i + 2, rows]
        y_sides = w[n, i + 1, pl.ds(PAD - 1, across)] + w[n, i + 1, pl.ds(PAD + 1, across)]
        before = jnp.where(lane == 0, 0.0, pltpu.roll(here, 1, 1))
        after = jnp.where(lane == depth - 1, 0.0, pltpu.roll(here, depth - 1, 1))
        return here, x_sides + y_sides + (before + after)

    def step(n, i):
        here, sides = around(n, i)
        w[n + 1, i + 1, rows] = keep[i] * here + cond[i] * sides

    for n in range(FINE_STEPS - 1):
        wait_faces(n)
        step(n, 0)
        step(n, planes - 1)
        send_faces(n + 1)
        lax.fori_loop(1, planes - 1, lambda i, c: (step(n, i), c)[1], 0, unroll=UNROLL)

    def finish(i):
        here, sides = around(FINE_STEPS - 1, i)
        out[0, i] = keep[i] * here / cond[i] + sides

    def reduce(j):
        mean = four(out.at[0], j)
        red[j] = jnp.where(is_top, mean, mean - rate[j] * old[j])

    def last_step(k):
        for q in (half - 1 - k, half + k):
            finish(2 * q)
            finish(2 * q + 1)
            for r in range(CUT):
                reduce(q * CUT + r)
        for r in range(CUT):
            red_copy(k * CUT + r).start()

    lax.fori_loop(0, half - 1, lambda k, c: (last_step(k), c)[1], 0)
    wait_faces(FINE_STEPS - 1)
    last_step(half - 1)
    vent_copy().wait_recv()

    def combine(c, _):
        j = own_chunk(c)
        mine = rate[j]
        his = jnp.exp(-FINE_STEPS * (four(loss, j) + mate_vent[0:1, :]))
        red_copy(c).wait_recv()
        low_rate, upper_rate = jnp.where(low, mine, his), jnp.where(low, his, mine)
        low_red, upper_red = jnp.where(low, red[j], mate_red[c]), jnp.where(low, mate_red[c], red[j])
        gain[c] = low_rate * upper_rate
        base[c] = low_red + low_rate * upper_red
        high_red[c] = upper_red
        high_rate[c] = upper_rate

        @pl.when(jnp.logical_not(has_upper))
        def _():
            chain_out[c] = low_red + low_rate * upper_red
            pl.when(has_lower)(lambda: chain_copy(c).start())

        return 0

    lax.fori_loop(0, chunks, combine, 0)

    def add_carry(j, carry):
        q, r = j // CUT, j % CUT
        moved = jnp.where(is_top, 0.0, rate[j] * (carry - old[j]))
        for i in (2 * q, 2 * q + 1):
            plane = out.at[0, i]
            for phase in range(2):
                pick = pl.ds(2 * part * r + phase, part, stride=2)
                plane[pick, :] = plane[pick, :] + moved

    def pass_on(c, entering):
        lower = high_red[c] + high_rate[c] * entering
        swap_out[c] = jnp.where(low, entering, lower)
        swap_copy(c).start()
        carried[c] = jnp.where(low, lower, entering)

    @pl.when(has_upper)
    def _():
        def link(c, _):
            chain_copy(c).wait_recv()
            entering = chain_in[c]
            chain_out[c] = base[c] + gain[c] * entering
            pl.when(has_lower)(lambda: chain_copy(c).start())
            pass_on(c, entering)
            return 0

        lax.fori_loop(0, chunks, link, 0)

    @pl.when(jnp.logical_not(has_upper))
    def _():
        def link(c, _):
            pass_on(c, jnp.zeros((part, depth), F32))
            return 0

        lax.fori_loop(0, chunks, link, 0)

    def own(c, _):
        add_carry(own_chunk(c), carried[c])
        return 0

    lax.fori_loop(0, chunks, own, 0)

    def close(c, _):
        swap_copy(c).wait_recv()
        add_carry(mate_chunk(c), swap_in[c])
        return 0

    lax.fori_loop(0, chunks, close, 0)

    vent_copy().wait_send()
    for n in range(FINE_STEPS):
        pl.when(has_left)(lambda: left_copy(n).wait_send())
        pl.when(has_right)(lambda: right_copy(n).wait_send())
    for k in range(chunks):
        red_copy(k).wait_send()
        pl.when(has_lower)(lambda: chain_copy(k).wait_send())
        swap_copy(k).wait_send()


def on_device(slabs, tiles, prior, material, probe, misfit, vent, conductance, drain):
    planes, across, depth = prior.shape[1:]
    pieces, chunks, part = planes // 2 * CUT, planes // 4 * CUT, across // 2 // CUT
    sensors = probe.shape[0]
    vmem, hbm = pl.BlockSpec(memory_space=pltpu.VMEM), pl.BlockSpec(memory_space=pltpu.HBM)
    whole = pltpu.VMEM((planes, across, depth), F32)
    quarter = pltpu.VMEM((pieces, part, depth), F32)
    eighth = pltpu.VMEM((chunks, part, depth), F32)
    small = pltpu.VMEM((8, depth), F32)
    dma = pltpu.SemaphoreType.DMA
    return pl.pallas_call(
        functools.partial(kernel, slabs, tiles),
        out_shape=jax.ShapeDtypeStruct(prior.shape, F32),
        in_specs=[hbm] * 7,
        out_specs=vmem,
        scratch_shapes=[
            pltpu.VMEM(prior.shape, F32), pltpu.VMEM(material.shape, jnp.int32),
            pltpu.VMEM((1, sensors), jnp.int32), pltpu.VMEM(misfit.shape, F32),
            pltpu.SMEM(vent.shape, F32), pltpu.SMEM(conductance.shape, F32), pltpu.SMEM(drain.shape, F32),
            dma((11,)),
            pltpu.VMEM((FINE_STEPS, planes + 2, across + 2 * PAD, depth), F32),
            whole, whole, whole, quarter, quarter, quarter,
            pltpu.VMEM((3, depth, sensors), BF16),
            small, small, eighth, eighth, eighth, eighth, eighth,
            eighth, eighth, eighth, eighth, eighth,
            dma((2,)), dma((FINE_STEPS, 2)), dma((FINE_STEPS, 2)),
            dma((chunks,)), dma((chunks,)), dma((chunks,)), dma((chunks,)), dma((chunks,)), dma((chunks,)),
        ],
        compiler_params=pltpu.CompilerParams(
            collective_id=0, has_side_effects=True, vmem_limit_bytes=60 * 1024 * 1024
        ),
    )(prior, material, probe.reshape(1, sensors), misfit, vent, conductance, drain)


def solution(mesh):
    in_specs = (
        P("tm", "space", None, None),
        P("space", None, None),
        P("space"),
        P("tm", "space"),
        P("tm"),
        P(),
        P(),
    )
    out_specs = P("tm", "space", None, None)
    run = functools.partial(on_device, mesh.shape["tm"], mesh.shape["space"])
    return jax.shard_map(run, mesh=mesh, in_specs=in_specs, out_specs=out_specs, check_vma=False)
```

```python
import functools

import jax
import jax.numpy as jnp
from jax import lax
from jax.experimental import pallas as pl
from jax.experimental.pallas import tpu as pltpu
from jax.sharding import PartitionSpec as P

FINE_STEPS = 4
PAD = 8
CUT = 2
UNROLL = 2
F32 = jnp.float32
BF16 = jnp.bfloat16


def lookup(rock, tables):
    bits = [(rock & (1 << b)) != 0 for b in range(3)]
    found = []
    for table in tables:
        level = table
        for bit in bits:
            level = [jnp.where(bit, level[2 * n + 1], level[2 * n]) for n in range(len(level) // 2)]
        found.append(level[0])
    return found


def kernel(
    slabs, tiles,
    prior_in, material_in, probe_in, misfit_in, conductance_in, drain_in, vent,
    out,
    prior, material, probe, misfit, conductance, drain, in_sem,
    w, cond, keep, loss, rate, old, red,
    seen, mate_vent, my_vent, mate_red, gain, base, high_red, high_rate,
    chain_in, chain_out, swap_out, swap_in, carried,
    vent_sem, halo_send, halo_recv, red_send, red_recv, chain_send, chain_recv, swap_send, swap_recv,
):
    t, p = lax.axis_index("tm"), lax.axis_index("space")
    planes, across, depth = prior.shape[1:]
    coarse = planes // 2
    half = coarse // 2
    chunks = half * CUT
    part = across // 2 // CUT
    inner = pl.ds(1, planes - 2)
    small = [(probe_in, probe), (misfit_in, misfit), (conductance_in, conductance), (drain_in, drain)]
    faces, body = [], []
    for i in (0, planes - 1):
        faces += [(prior_in.at[0, i], prior.at[0, i]), (material_in.at[i], material.at[i])]
    body += [(material_in.at[inner], material.at[inner]), (prior_in.at[0, inner], prior.at[0, inner])]
    loads = [pltpu.make_async_copy(a, b, in_sem.at[n]) for n, (a, b) in enumerate(small + faces + body)]
    for load in loads:
        load.start()
    rows = pl.ds(PAD, across)
    low = lax.rem(t, 2) == 0
    mate = jnp.where(low, t + 1, t - 1)
    has_lower, has_upper = t >= 2, t < slabs - 2
    has_left, has_right = p > 0, p < tiles - 1
    is_top = t == slabs - 1

    def own_chunk(c):
        k, r = c // CUT, c % CUT
        return jnp.where(low, half - 1 - k, half + k) * CUT + r

    def mate_chunk(c):
        k, r = c // CUT, c % CUT
        return jnp.where(low, half + k, half - 1 - k) * CUT + r

    barrier = pltpu.get_barrier_semaphore()

    def greet(axis, index):
        pl.semaphore_signal(barrier, inc=1, device_id={axis: index}, device_id_type=pl.DeviceIdType.MESH)

    greet("tm", mate)
    pl.when(has_lower)(lambda: greet("tm", t - 2))
    pl.when(has_upper)(lambda: greet("tm", t + 2))
    pl.when(has_left)(lambda: greet("space", p - 1))
    pl.when(has_right)(lambda: greet("space", p + 1))

    def send(src, dst, send_sem, recv_sem, axis, index):
        return pltpu.make_async_remote_copy(
            src_ref=src, dst_ref=dst, send_sem=send_sem, recv_sem=recv_sem,
            device_id={axis: index}, device_id_type=pl.DeviceIdType.MESH,
        )

    def vent_copy():
        return send(my_vent, mate_vent, vent_sem.at[0], vent_sem.at[1], "tm", mate)

    def left_copy(n):
        return send(w.at[n, 1, rows], w.at[n, planes + 1, rows], halo_send.at[n, 0], halo_recv.at[n, 0], "space", p - 1)

    def right_copy(n):
        return send(w.at[n, planes, rows], w.at[n, 0, rows], halo_send.at[n, 1], halo_recv.at[n, 1], "space", p + 1)

    def red_copy(k):
        return send(red.at[mate_chunk(k)], mate_red.at[k], red_send.at[k], red_recv.at[k], "tm", mate)

    def chain_copy(k):
        return send(chain_out.at[k], chain_in.at[k], chain_send.at[k], chain_recv.at[k], "tm", t - 2)

    def swap_copy(k):
        return send(swap_out.at[k], swap_in.at[k], swap_send.at[k], swap_recv.at[k], "tm", mate)

    edge = jnp.zeros((PAD, depth), F32)

    def clear(i, _):
        for n in range(FINE_STEPS):
            w[n, i + 1, pl.ds(0, PAD)] = edge
            w[n, i + 1, pl.ds(PAD + across, PAD)] = edge
        return 0

    lax.fori_loop(0, planes, clear, 0)

    @pl.when(jnp.logical_not(has_left))
    def _():
        for n in range(FINE_STEPS):
            w[n, 0, rows] = jnp.zeros((across, depth), F32)

    @pl.when(jnp.logical_not(has_right))
    def _():
        for n in range(FINE_STEPS):
            w[n, planes + 1, rows] = jnp.zeros((across, depth), F32)

    for load in loads[: len(small)]:
        load.wait()
    extra = vent[0]
    cond_of = [conductance[m] for m in range(conductance.shape[0])]
    drain_of = [drain[m] for m in range(drain.shape[0])]

    cell = probe[...] - p * (planes * across * depth)
    cell_row, cell_lane = cell // depth, lax.rem(cell, depth)
    amount = misfit[...]
    first = amount.astype(BF16)
    rest = amount - first.astype(F32)
    second = rest.astype(BF16)
    third = rest - second.astype(F32)
    place = lax.broadcasted_iota(jnp.int32, (depth, cell.shape[1]), 0) == cell_lane
    for n, term in enumerate((first.astype(F32), second.astype(F32), third)):
        seen[n] = jnp.where(place, term, 0.0).astype(BF16)

    def seed(i):
        number = lax.broadcasted_iota(jnp.int32, (across, cell.shape[1]), 0) + i * across
        hit = jnp.where(number == cell_row, 1.0, 0.0).astype(BF16)
        added = sum(
            lax.dot_general(hit, seen[n], (((1,), (1,)), ((), ())), preferred_element_type=F32)
            for n in range(3)
        )
        c, l = lookup(material[i], (cond_of, drain_of))
        cond[i] = c
        loss[i] = l
        keep[i] = 1.0 - 6.0 * c - (l + extra)
        w[0, i + 1, rows] = c * (prior[0, i] + added)

    for load in loads[len(small) : len(small) + len(faces)]:
        load.wait()
    seed(0)
    seed(planes - 1)
    my_vent[...] = jnp.full(my_vent.shape, extra, F32)
    count = 1 + has_lower.astype(jnp.int32) + has_upper.astype(jnp.int32)
    count = count + has_left.astype(jnp.int32) + has_right.astype(jnp.int32)
    pl.semaphore_wait(barrier, count)

    def send_faces(n):
        pl.when(has_left)(lambda: left_copy(n).start())
        pl.when(has_right)(lambda: right_copy(n).start())

    def wait_faces(n):
        pl.when(has_right)(lambda: left_copy(n).wait_recv())
        pl.when(has_left)(lambda: right_copy(n).wait_recv())

    send_faces(0)
    vent_copy().start()

    for load in loads[len(small) + len(faces) :]:
        load.wait()
    lax.fori_loop(1, planes - 1, lambda i, c: (seed(i), c)[1], 0, unroll=2)

    def four(ref, j):
        q, r = j // CUT, j % CUT
        start = 2 * part * r
        even, odd = pl.ds(start, part, stride=2), pl.ds(start + 1, part, stride=2)
        a, b = ref.at[2 * q], ref.at[2 * q + 1]
        return 0.25 * ((a[even, :] + b[even, :]) + (a[odd, :] + b[odd, :]))

    def prepare(j, _):
        rate[j] = jnp.exp(-FINE_STEPS * (four(loss, j) + extra))
        old[j] = four(prior.at[0], j)
        return 0

    lax.fori_loop(0, coarse * CUT, prepare, 0, unroll=2)

    lane = lax.broadcasted_iota(jnp.int32, (across, depth), 1)

    def around(n, i):
        here = w[n, i + 1, rows]
        x_sides = w[n, i, rows] + w[n, i + 2, rows]
        y_sides = w[n, i + 1, pl.ds(PAD - 1, across)] + w[n, i + 1, pl.ds(PAD + 1, across)]
        before = jnp.where(lane == 0, 0.0, pltpu.roll(here, 1, 1))
        after = jnp.where(lane == depth - 1, 0.0, pltpu.roll(here, depth - 1, 1))
        return here, x_sides + y_sides + (before + after)

    def step(n, i):
        here, sides = around(n, i)
        w[n + 1, i + 1, rows] = keep[i] * here + cond[i] * sides

    for n in range(FINE_STEPS - 1):
        wait_faces(n)
        step(n, 0)
        step(n, planes - 1)
        send_faces(n + 1)
        lax.fori_loop(1, planes - 1, lambda i, c: (step(n, i), c)[1], 0, unroll=UNROLL)

    def finish(i):
        here, sides = around(FINE_STEPS - 1, i)
        out[0, i] = keep[i] * here / cond[i] + sides

    def reduce(j):
        mean = four(out.at[0], j)
        red[j] = jnp.where(is_top, mean, mean - rate[j] * old[j])

    def last_step(k):
        for q in (half - 1 - k, half + k):
            finish(2 * q)
            finish(2 * q + 1)
            for r in range(CUT):
                reduce(q * CUT + r)
        for r in range(CUT):
            red_copy(k * CUT + r).start()

    lax.fori_loop(0, half - 1, lambda k, c: (last_step(k), c)[1], 0)
    wait_faces(FINE_STEPS - 1)
    last_step(half - 1)
    vent_copy().wait_recv()

    def combine(c, _):
        j = own_chunk(c)
        mine = rate[j]
        his = jnp.exp(-FINE_STEPS * (four(loss, j) + mate_vent[0:1, :]))
        red_copy(c).wait_recv()
        low_rate, upper_rate = jnp.where(low, mine, his), jnp.where(low, his, mine)
        low_red, upper_red = jnp.where(low, red[j], mate_red[c]), jnp.where(low, mate_red[c], red[j])
        gain[c] = low_rate * upper_rate
        base[c] = low_red + low_rate * upper_red
        high_red[c] = upper_red
        high_rate[c] = upper_rate

        @pl.when(jnp.logical_not(has_upper))
        def _():
            chain_out[c] = low_red + low_rate * upper_red
            pl.when(has_lower)(lambda: chain_copy(c).start())

        return 0

    lax.fori_loop(0, chunks, combine, 0)

    def add_carry(j, carry):
        q, r = j // CUT, j % CUT
        moved = jnp.where(is_top, 0.0, rate[j] * (carry - old[j]))
        for i in (2 * q, 2 * q + 1):
            plane = out.at[0, i]
            for phase in range(2):
                pick = pl.ds(2 * part * r + phase, part, stride=2)
                plane[pick, :] = plane[pick, :] + moved

    def pass_on(c, entering):
        lower = high_red[c] + high_rate[c] * entering
        swap_out[c] = jnp.where(low, entering, lower)
        swap_copy(c).start()
        carried[c] = jnp.where(low, lower, entering)

    @pl.when(has_upper)
    def _():
        def link(c, _):
            chain_copy(c).wait_recv()
            entering = chain_in[c]
            chain_out[c] = base[c] + gain[c] * entering
            pl.when(has_lower)(lambda: chain_copy(c).start())
            pass_on(c, entering)
            return 0

        lax.fori_loop(0, chunks, link, 0)

    @pl.when(jnp.logical_not(has_upper))
    def _():
        def link(c, _):
            pass_on(c, jnp.zeros((part, depth), F32))
            return 0

        lax.fori_loop(0, chunks, link, 0)

    def own(c, _):
        add_carry(own_chunk(c), carried[c])
        return 0

    lax.fori_loop(0, chunks, own, 0)

    def close(c, _):
        swap_copy(c).wait_recv()
        add_carry(mate_chunk(c), swap_in[c])
        return 0

    lax.fori_loop(0, chunks, close, 0)

    vent_copy().wait_send()
    for n in range(FINE_STEPS):
        pl.when(has_left)(lambda: left_copy(n).wait_send())
        pl.when(has_right)(lambda: right_copy(n).wait_send())
    for k in range(chunks):
        red_copy(k).wait_send()
        pl.when(has_lower)(lambda: chain_copy(k).wait_send())
        swap_copy(k).wait_send()


def on_device(slabs, tiles, prior, material, probe, misfit, vent, conductance, drain):
    planes, across, depth = prior.shape[1:]
    pieces, chunks, part = planes // 2 * CUT, planes // 4 * CUT, across // 2 // CUT
    sensors = probe.shape[0]
    vmem, hbm = pl.BlockSpec(memory_space=pltpu.VMEM), pl.BlockSpec(memory_space=pltpu.HBM)
    whole = pltpu.VMEM((planes, across, depth), F32)
    quarter = pltpu.VMEM((pieces, part, depth), F32)
    eighth = pltpu.VMEM((chunks, part, depth), F32)
    small = pltpu.VMEM((8, depth), F32)
    dma = pltpu.SemaphoreType.DMA
    return pl.pallas_call(
        functools.partial(kernel, slabs, tiles),
        out_shape=jax.ShapeDtypeStruct(prior.shape, F32),
        in_specs=[hbm] * 6 + [pl.BlockSpec(memory_space=pltpu.SMEM)],
        out_specs=vmem,
        scratch_shapes=[
            pltpu.VMEM(prior.shape, F32), pltpu.VMEM(material.shape, jnp.int32),
            pltpu.VMEM((1, sensors), jnp.int32), pltpu.VMEM(misfit.shape, F32),
            pltpu.SMEM(conductance.shape, F32), pltpu.SMEM(drain.shape, F32),
            dma((10,)),
            pltpu.VMEM((FINE_STEPS, planes + 2, across + 2 * PAD, depth), F32),
            whole, whole, whole, quarter, quarter, quarter,
            pltpu.VMEM((3, depth, sensors), BF16),
            small, small, eighth, eighth, eighth, eighth, eighth,
            eighth, eighth, eighth, eighth, eighth,
            dma((2,)), dma((FINE_STEPS, 2)), dma((FINE_STEPS, 2)),
            dma((chunks,)), dma((chunks,)), dma((chunks,)), dma((chunks,)), dma((chunks,)), dma((chunks,)),
        ],
        compiler_params=pltpu.CompilerParams(
            collective_id=0, has_side_effects=True, vmem_limit_bytes=48 * 1024 * 1024
        ),
    )(*[
        pltpu.with_memory_space_constraint(array, pltpu.HBM)
        for array in (prior, material, probe.reshape(1, sensors), misfit, conductance, drain)
    ], vent)


def solution(mesh):
    in_specs = (
        P("tm", "space", None, None),
        P("space", None, None),
        P("space"),
        P("tm", "space"),
        P("tm"),
        P(),
        P(),
    )
    out_specs = P("tm", "space", None, None)
    run = functools.partial(on_device, mesh.shape["tm"], mesh.shape["space"])
    return jax.shard_map(run, mesh=mesh, in_specs=in_specs, out_specs=out_specs, check_vma=False)
```
